32 devices in a mesh: dp: 8 (over z, core), mp: 4 (over y, x).
Axes of the slice: x: 2, y: 2, z: 4, core: 2. Of those that a mesh axis runs over, the one named last changes fastest.
Arguments:
- patches: bfloat16 [16, 1568, 1536], P('dp', 'mp'), parts along dimension 0, may hold values from -64 to 64
- visible: int32 [16, 157], P('dp'), parts along dimension 0, may hold values from 0 to 1567, as said below
- embed_weight: bfloat16 [1536, 6144], P(None, 'mp'), may hold values from -4 to 4
- embed_bias: bfloat16 [6144], P('mp'), may hold values from -3 to 3
- norm_gain: bfloat16 [6144], P('mp'), may hold values from 0.099609375 to 1.8984375
- qkv_weight: bfloat16 [6144, 3, 4096], P(None, None, 'mp'), may hold values from -0.078125 to 0.078125
- query_gain: float32 [4096], P('mp'), may hold values from 0.5 to 20
- key_gain: float32 [4096], P('mp'), may hold values from 0.5 to 20
Outputs:
- context: bfloat16 [16, 157, 4096], P('dp', None, 'mp'), parts along dimension 0
The draws below stay inside these ranges and needn't reach their ends.
There are 8 independent parts, one for each index of `dp`. The reference program is written for one: setup_inputs(seed, part) draws one part's arguments, and reference() takes and returns one part's arrays. A program takes and returns all parts, laid end to end along the dimension named above; an argument that names none is the same for every part. Nothing has to cross between parts.
Inputs may be any that keep to these rules, and one draw needn't show every extreme that they name: `visible`: within a clip the entries are distinct; 0 and 1567 are among them.
All inputs are finite; a program needn't handle non-finite values.
Results may differ from the reference program's by a relative error of at most 0.033.
Values may be sent and summed in bfloat16 or wider, within the bound.
A program may use at most 192 MiB of HBM per device.

```python
import math
import jax
import jax.numpy as jnp
from jax import lax

CLIPS = 2
TUBES = 1568
VIS = 157
PD = 1536
D = 6144
HEADS = 32
HS = 128


def draw_patches(key, part):
    key = jax.random.fold_in(key, 11)
    first, second = jax.random.split(key, 2)
    base = jax.random.truncated_normal(first, -4.0, 4.0, (CLIPS, TUBES, PD), jnp.float32)
    spread = jnp.exp(jax.random.uniform(second, (CLIPS, TUBES, 1), jnp.float32) * math.log(10.0))
    return (base * spread).astype(jnp.bfloat16)


def draw_visible(key, part):
    key = jax.random.fold_in(key, 23)

    def one_clip(subkey):
        first, second = jax.random.split(subkey)
        inner = jax.random.permutation(first, TUBES - 2)[:VIS - 2].astype(jnp.int32) + 1
        chosen = jnp.concatenate([inner, jnp.array([0, TUBES - 1], jnp.int32)])
        return chosen[jax.random.permutation(second, VIS)]
    return jax.vmap(one_clip)(jax.random.split(key, CLIPS)).astype(jnp.int32)


def draw_embed_weight(key, part):
    key = jax.random.fold_in(key, 37)
    first, second = jax.random.split(key)
    columns = jnp.arange(D, dtype=jnp.float32)
    rising = jnp.power(jnp.float32(10.0), columns / D - 0.5)
    rough = jnp.exp(jax.random.uniform(second, (1, D), jnp.float32, math.log(0.7), math.log(1.4)))
    base = jax.random.truncated_normal(first, -4.0, 4.0, (PD, D), jnp.float32)
    return (base * rising * rough / math.sqrt(PD)).astype(jnp.bfloat16)


def gain_table(key):
    first = jax.random.fold_in(key, 0)
    channel = jnp.exp(jax.random.uniform(first, (HEADS, HS), jnp.float32, math.log(0.6), math.log(2.5)))
    return channel.reshape(HEADS * HS)


def draw_query_gain(key, part):
    key = jax.random.fold_in(key, 41)
    return gain_table(key)


def draw_key_gain(key, part):
    key = jax.random.fold_in(key, 53)
    return gain_table(key)


def block_scale(rng, shape, pieces, least, largest):
    level, own = 1.0, jax.random.fold_in(rng, 6)
    for position, blocks in pieces:
        heights = jnp.exp(jax.random.uniform(jax.random.fold_in(own, position), (blocks,), jnp.float32, least / len(pieces), largest / len(pieces)))
        level = level * jnp.repeat(heights, shape[position] // blocks).reshape([-1 if axis == position else 1 for axis in range(len(shape))])
    return level


def gaussian(stream_key, extent, scale, bound, shards=(), held_as=jnp.bfloat16):
    level = block_scale(stream_key, extent, shards, -0.22, 0.18) if shards else 1.0
    result = jax.random.normal(stream_key, extent, jnp.float32) * scale * level
    return jnp.minimum(jnp.maximum(result, -bound), bound).astype(held_as)


def setup_inputs(seed: int = 0, part: int = 0) -> dict:
    streams_of = jax.random.split(jax.random.key(seed), 9)
    own_keys = jax.random.split(jax.random.fold_in(streams_of[8], part), 9)
    patches = draw_patches(jax.random.fold_in(jax.random.fold_in(streams_of[8], part), 71), part)
    visible = draw_visible(jax.random.fold_in(jax.random.fold_in(streams_of[8], part), 71), part)
    embed_weight = draw_embed_weight(jax.random.fold_in(streams_of[8], 71), part)
    embed_bias = gaussian(streams_of[3], (D,), 0.5, 3.0, ((0, 4),))
    norm_gain = jnp.clip(1.0 + 0.18 * jax.random.normal(streams_of[4], (D,), jnp.float32), 0.099609375, 1.8984375).astype(jnp.bfloat16)
    qkv_weight = gaussian(streams_of[5], (D, 3, HEADS * HS), D ** -0.5, 0.078125, ((2, 4),))
    query_gain = draw_query_gain(jax.random.fold_in(streams_of[8], 71), part)
    key_gain = draw_key_gain(jax.random.fold_in(streams_of[8], 71), part)
    return {"patches": patches, "visible": visible, "embed_weight": embed_weight, "embed_bias": embed_bias, "norm_gain": norm_gain, "qkv_weight": qkv_weight, "query_gain": query_gain, "key_gain": key_gain}


eps = 1e-06

def positions(index, columns):
    rate = jnp.power(jnp.float32(10000.0), -(2 * (columns // 2)).astype(jnp.float32) / D)
    angle = index.astype(jnp.float32)[..., None] * rate
    return jnp.where(columns % 2 == 0, jnp.sin(angle), jnp.cos(angle))

def normalize(values, gain):
    width = values.shape[-1]
    row_mean = lax.optimization_barrier(jnp.sum(values, -1, keepdims=True)) / width
    row_var = lax.optimization_barrier(jnp.sum(values * values, -1, keepdims=True)) / width - row_mean * row_mean
    return (values - row_mean) * lax.rsqrt(row_var + eps) * gain

def reference(patches, visible, embed_weight, embed_bias, norm_gain, qkv_weight, query_gain, key_gain):
    picked = jnp.take_along_axis(patches, visible.astype(jnp.int32)[:, :, None], axis=1)
    flat = picked.reshape(CLIPS * VIS, PD)
    embedded = jnp.dot(flat, embed_weight, preferred_element_type=jnp.float32).reshape(CLIPS, VIS, D)
    columns = jnp.arange(D, dtype=jnp.int32)
    tokens = (embedded + embed_bias.astype(jnp.float32) + positions(visible, columns)).astype(jnp.bfloat16)
    normed = normalize(tokens.astype(jnp.float32), norm_gain.astype(jnp.float32)).astype(jnp.bfloat16)
    projected = jnp.dot(normed.reshape(CLIPS * VIS, D), qkv_weight.reshape(D, 3 * HEADS * HS), preferred_element_type=jnp.float32).astype(jnp.bfloat16)
    projected = projected.reshape(CLIPS, VIS, 3, HEADS, HS)
    queries = projected[:, :, 0].astype(jnp.float32)
    keys = projected[:, :, 1].astype(jnp.float32)
    values = projected[:, :, 2].astype(jnp.float32)
    query_normed = normalize(queries, query_gain.reshape(HEADS, HS)).astype(jnp.bfloat16).astype(jnp.float32)
    key_normed = normalize(keys, key_gain.reshape(HEADS, HS)).astype(jnp.bfloat16).astype(jnp.float32)
    scores = jnp.einsum('cqhd,ckhd->chqk', query_normed, key_normed) / jnp.sqrt(jnp.float32(HS))
    probabilities = jax.nn.softmax(scores, axis=-1).astype(jnp.bfloat16).astype(jnp.float32)
    context = jnp.einsum('chqk,ckhd->cqhd', probabilities, values)
    return context.reshape(CLIPS, VIS, HEADS * HS).astype(jnp.bfloat16)
```

```python
import functools

import jax
import jax.numpy as jnp
import numpy as np
from jax import lax
from jax.experimental import pallas as pl
from jax.experimental.pallas import tpu as pltpu
from jax.sharding import PartitionSpec as P

D = 6144
HS = 128


eps = 1e-06


def positions(index, columns):
    rate = jnp.power(jnp.float32(10000.0), -(2 * (columns // 2)).astype(jnp.float32) / D)
    angle = index.astype(jnp.float32)[..., None] * rate
    return jnp.where(columns % 2 == 0, jnp.sin(angle), jnp.cos(angle))


def normalize(values, gain):
    width = values.shape[-1]
    row_mean = jnp.sum(values, -1, keepdims=True) / width
    row_var = jnp.sum(values * values, -1, keepdims=True) / width - row_mean * row_mean
    return (values - row_mean) * lax.rsqrt(row_var + eps) * gain


def local_generic(patches, visible, embed_weight, embed_bias, norm_gain, qkv_weight, query_gain, key_gain):
    clip_count, local_tubes, patch_width = patches.shape
    seen = visible.shape[1]
    row_count = clip_count * seen
    feature_local = embed_weight.shape[1]
    head_cols = qkv_weight.shape[2]
    heads_local = head_cols // HS
    first_tube = lax.axis_index("mp") * local_tubes
    selector = (
        visible[:, :, None] - first_tube == jnp.arange(local_tubes, dtype=jnp.int32)[None, None, :]
    ).astype(jnp.bfloat16)
    picked = (
        jnp.einsum("cvt,ctp->cvp", selector, patches, preferred_element_type=jnp.float32)
        .reshape(row_count, patch_width)
        .astype(jnp.bfloat16)
    )
    shared = lax.psum(picked, "mp").astype(jnp.float32).astype(jnp.bfloat16)
    embedded = jnp.dot(shared, embed_weight, preferred_element_type=jnp.float32)
    columns = lax.axis_index("mp") * feature_local + jnp.arange(feature_local, dtype=jnp.int32)
    placed = positions(visible, columns).reshape(row_count, feature_local)
    tokens = (embedded + embed_bias.astype(jnp.float32) + placed).astype(jnp.bfloat16)
    weight_flat = qkv_weight.reshape(qkv_weight.shape[0], 3 * head_cols)
    token_float = tokens.astype(jnp.float32)
    row_sums = lax.psum((jnp.sum(token_float, 1), jnp.sum(token_float * token_float, 1)), "mp")
    row_mean = row_sums[0] / D
    row_var = row_sums[1] / D - row_mean * row_mean
    normed = (
        (token_float - row_mean[:, None])
        * lax.rsqrt(row_var + eps)[:, None]
        * norm_gain.astype(jnp.float32)
    ).astype(jnp.bfloat16)
    projected = jnp.dot(
        lax.all_gather(normed, "mp", axis=1, tiled=True),
        weight_flat,
        preferred_element_type=jnp.float32,
    )
    projected = projected.astype(jnp.bfloat16).reshape(clip_count, seen, 3, heads_local, HS)
    queries = projected[:, :, 0].astype(jnp.float32)
    keys_local = projected[:, :, 1].astype(jnp.float32)
    values_local = projected[:, :, 2]
    query_normed = normalize(queries, query_gain.reshape(heads_local, HS)).astype(jnp.bfloat16)
    key_normed = normalize(keys_local, key_gain.reshape(heads_local, HS)).astype(jnp.bfloat16)
    scores = jnp.einsum(
        "cqhd,ckhd->chqk", query_normed, key_normed, preferred_element_type=jnp.float32
    ) / jnp.sqrt(jnp.float32(HS))
    probabilities = jax.nn.softmax(scores, axis=-1).astype(jnp.bfloat16)
    context = jnp.einsum(
        "chqk,ckhd->cqhd", probabilities, values_local, preferred_element_type=jnp.float32
    )
    return context.reshape(clip_count, seen, head_cols).astype(jnp.bfloat16)


MESH = pl.DeviceIdType.MESH
NEG = -1e30


def turn_table():
    columns = np.arange(D)
    turns = 10000.0 ** (-2.0 * (columns // 2) / D) / (2 * np.pi)
    exponent = np.floor(np.log2(turns))
    step = 2.0 ** (exponent - 11)
    high = np.round(turns / step) * step
    low = turns - high
    phase = np.where(columns % 2 == 0, 0.0, 0.25)
    table = np.zeros((8, D), np.float32)
    table[0], table[1], table[2] = high, low, phase
    return table


def sine_of_turns(turn):
    size = jnp.abs(turn)
    size = jnp.minimum(size, 0.5 - size)
    x = jnp.where(turn < 0, -size, size) * jnp.float32(2 * np.pi)
    y = x * x
    s = jnp.float32(2.7557319e-06) - jnp.float32(2.5052108e-08) * y
    s = s * y - jnp.float32(1.9841270e-04)
    s = s * y + jnp.float32(8.3333333e-03)
    s = s * y - jnp.float32(1.6666667e-01)
    return x + x * y * s


def kernel(
    sizes,
    visible_ref, par_ref, table_ref, patches_hbm, embed_hbm, qkv_hbm,
    out_ref,
    patch, embed, weight, masked, part, picked, placed, tokens, stats, gains, normed, total,
    local_sem, gain_send, gain_recv, part_send, part_recv, pick_send, pick_recv,
    stat_send, stat_recv, token_send, token_recv,
):
    clips, rows, seen, quarter, width, heads = sizes
    half = rows // 2
    me = lax.axis_index("mp")
    dp = lax.axis_index("dp")
    xn = me + 1 - 2 * (me % 2)
    yn = me + 2 - 4 * (me // 2)
    dg = 3 - me
    peers = (xn, yn, dg)

    def push(src, dst, send, recv, peer):
        return pltpu.make_async_remote_copy(
            src_ref=src, dst_ref=dst, send_sem=send, recv_sem=recv,
            device_id=(dp, peer), device_id_type=MESH,
        )

    patch_copies = [
        pltpu.make_async_copy(patches_hbm.at[c], patch.at[c], local_sem.at[c]) for c in range(clips)
    ]
    embed_copy = pltpu.make_async_copy(embed_hbm, embed, local_sem.at[2])
    for copy in patch_copies:
        copy.start()
    embed_copy.start()
    barrier = pltpu.get_barrier_semaphore()
    for peer in peers:
        pl.semaphore_signal(barrier, inc=1, device_id=(dp, peer), device_id_type=MESH)
    order = (me, xn, yn, dg)
    weight_copies = []
    for k, s in enumerate(order):
        span = pl.ds(pl.multiple_of(s * width, width), width)
        copy = pltpu.make_async_copy(
            qkv_hbm.at[:, span, :], weight.at[:, span, :], local_sem.at[3 + k]
        )
        copy.start()
        weight_copies.append(copy)
    gains[me] = par_ref[1:2, :]

    sends = []

    def select(c):
        patch_copies[c].wait()
        tubes = patch.shape[1]
        first = me * tubes
        spot = lax.broadcasted_iota(jnp.int32, (rows, tubes), 1) + first
        pick = (visible_ref[pl.ds(c * rows, rows), :] == spot).astype(jnp.float32).astype(jnp.bfloat16)
        for q in range(4):
            masked[c, q] = jnp.dot(
                pick, patch[c, :, q * quarter:(q + 1) * quarter], preferred_element_type=jnp.float32
            ).astype(jnp.bfloat16)

    part_copies = [
        [
            push(masked.at[c, peer], part.at[c, k], part_send.at[c, k], part_recv.at[c, k], peer)
            for k, peer in enumerate(peers)
        ]
        for c in range(clips)
    ]

    def spread(buffer, c, send, recv):
        low, high = pl.ds(0, half), pl.ds(half, half)

        def one(src, span, k, peer):
            ref = buffer.at[c, src, span, :]
            return push(ref, ref, send.at[c, k], recv.at[c, k], peer)

        own = [one(me, low, 0, xn), one(me, high, 3, yn), one(me, high, 1, xn), one(me, low, 2, yn)]
        forward = {0: one(xn, low, 4, yn), 3: one(yn, high, 5, xn)}
        arrive = [
            one(xn, low, 0, xn), one(xn, high, 1, xn), one(yn, low, 2, yn), one(yn, high, 3, yn),
            one(dg, low, 4, yn), one(dg, high, 5, xn),
        ]
        return own, forward, arrive

    pick_plan = [spread(picked, c, pick_send, pick_recv) for c in range(clips)]
    token_plan = [spread(tokens, c, token_send, token_recv) for c in range(clips)]

    def begin(plan):
        for copy in plan[0]:
            copy.start()

    def relay(plan):
        for k in (0, 3):
            plan[2][k].wait_recv()
            plan[1][k].start()

    select(0)
    pl.semaphore_wait(barrier, 3)
    for copy in part_copies[0]:
        copy.start()
    gain_copies = [
        push(gains.at[me], gains.at[me], gain_send.at[k], gain_recv.at[k], peer)
        for k, peer in enumerate(peers)
    ]
    for copy in gain_copies:
        copy.start()
    select(1)
    for copy in part_copies[1]:
        copy.start()

    here = pl.ds(pl.multiple_of(me * width, width), width)
    for c in range(clips):
        @pl.loop(0, rows // 16)
        def _(r, c=c):
            span = pl.ds(pl.multiple_of(r * 16, 16), 16)
            vspan = pl.ds(pl.multiple_of(c * rows + r * 16, 16), 16)
            index = visible_ref[vspan, :].astype(jnp.float32)
            coarse = index * table_ref[0:1, here]
            turn = (coarse - jnp.round(coarse)) + index * table_ref[1:2, here] + table_ref[2:3, here]
            turn = turn - jnp.round(turn)
            placed[c, span, :] = sine_of_turns(turn) + par_ref[0:1, :]

    for c in range(clips):
        for copy in part_copies[c]:
            copy.wait_recv()
        picked[c, me] = (masked[c, me] + part[c, 0]) + (part[c, 1] + part[c, 2])
        begin(pick_plan[c])

    ones = jnp.ones((8, width), jnp.bfloat16)
    rowdims = (((1,), (1,)), ((), ()))
    stat_copies = [
        [
            push(stats.at[c, me], stats.at[c, me], stat_send.at[c, k], stat_recv.at[c, k], peer)
            for k, peer in enumerate(peers)
        ]
        for c in range(clips)
    ]
    for c in range(clips):
        relay(pick_plan[c])
        for k in (1, 2, 4, 5):
            pick_plan[c][2][k].wait_recv()
        if c == 0:
            embed_copy.wait()
        for n in range(width // 512):
            cols = slice(n * 512, (n + 1) * 512)
            value = placed[c, :, cols]
            for q in range(4):
                value += jnp.dot(
                    picked[c, q], embed[q * quarter:(q + 1) * quarter, cols],
                    preferred_element_type=jnp.float32,
                )
            tokens[c, me, :, cols] = value.astype(jnp.bfloat16)
        begin(token_plan[c])
        value = tokens[c, me]
        wide = value.astype(jnp.float32)
        square = wide * wide
        top = square.astype(jnp.bfloat16)
        rest = (square - top.astype(jnp.float32)).astype(jnp.bfloat16)
        sums = lax.dot_general(ones, value, rowdims, preferred_element_type=jnp.float32)
        squares = lax.dot_general(ones, top, rowdims, preferred_element_type=jnp.float32)
        squares += lax.dot_general(ones, rest, rowdims, preferred_element_type=jnp.float32)
        stats[c, me, 0:8, 0:rows] = sums
        stats[c, me, 8:16, 0:rows] = squares
        for copy in stat_copies[c]:
            copy.start()

    def row_stats(c):
        for copy in stat_copies[c]:
            copy.wait_recv()
        both = (stats[c, 0] + stats[c, 1]) + (stats[c, 2] + stats[c, 3])
        both = both[:, 0:rows]
        mean = both[0:8, :] / D
        scale = lax.rsqrt(both[8:16, :] / D - mean * mean + eps)
        return jnp.transpose(mean)[:, 0:1], jnp.transpose(scale)[:, 0:1]

    def project(c, k, mean, scale):
        s = order[k]
        normed[...] = (
            (tokens[c, s].astype(jnp.float32) - mean) * scale * gains[s]
        ).astype(jnp.bfloat16)
        if c == 0:
            weight_copies[k].wait()
        span = pl.ds(pl.multiple_of(s * width, width), width)
        block = 512
        per = weight.shape[2] // block

        @pl.loop(0, 3 * per)
        def _(t):
            j, n = t // per, t % per
            cols = pl.ds(pl.multiple_of(n * block, block), block)
            value = jnp.dot(normed[...], weight[j, span, cols], preferred_element_type=jnp.float32)
            if k == 0:
                total[c, j, :, cols] = value
            else:
                total[c, j, :, cols] += value

    def head_norm(value, gain):
        value = value.astype(jnp.bfloat16).astype(jnp.float32)
        mean = jnp.sum(value, -1, keepdims=True) / HS
        var = jnp.sum(value * value, -1, keepdims=True) / HS - mean * mean
        return ((value - mean) * lax.rsqrt(var + eps) * gain).astype(jnp.bfloat16)

    valid = lax.broadcasted_iota(jnp.int32, (rows, rows), 1) < seen

    def attend(c):
        for h in range(heads):
            cols = slice(h * HS, (h + 1) * HS)
            query = head_norm(total[c, 0, :, cols], par_ref[2:3, cols])
            key = head_norm(total[c, 1, :, cols], par_ref[3:4, cols])
            scores = lax.dot_general(query, key, rowdims, preferred_element_type=jnp.float32)
            scores = jnp.where(valid, scores * jnp.float32(1 / np.sqrt(HS)), NEG)
            weights = jnp.exp(scores - jnp.max(scores, -1, keepdims=True))
            amount = jnp.sum(weights, -1, keepdims=True)
            context = jnp.dot(
                weights.astype(jnp.bfloat16), total[c, 2, :, cols].astype(jnp.bfloat16),
                preferred_element_type=jnp.float32,
            )
            out_ref[c * rows:(c + 1) * rows, cols] = (context / amount).astype(jnp.bfloat16)

    for copy in gain_copies:
        copy.wait_recv()
    mean0, scale0 = row_stats(0)
    project(0, 0, mean0, scale0)
    relay(token_plan[0])
    token_plan[0][2][1].wait_recv()
    project(0, 1, mean0, scale0)
    token_plan[0][2][2].wait_recv()
    project(0, 2, mean0, scale0)
    mean1, scale1 = row_stats(1)
    project(1, 0, mean1, scale1)
    token_plan[0][2][4].wait_recv()
    token_plan[0][2][5].wait_recv()
    project(0, 3, mean0, scale0)
    relay(token_plan[1])
    attend(0)
    token_plan[1][2][1].wait_recv()
    project(1, 1, mean1, scale1)
    token_plan[1][2][2].wait_recv()
    project(1, 2, mean1, scale1)
    token_plan[1][2][4].wait_recv()
    token_plan[1][2][5].wait_recv()
    project(1, 3, mean1, scale1)
    attend(1)

    for copy in gain_copies:
        copy.wait_send()
    for c in range(clips):
        for copy in part_copies[c] + stat_copies[c]:
            copy.wait_send()
        for plan in (pick_plan[c], token_plan[c]):
            for copy in plan[0] + [plan[1][0], plan[1][3]]:
                copy.wait_send()


def local_square(patches, visible, embed_weight, embed_bias, norm_gain, qkv_weight, query_gain, key_gain):
    clips, tubes, patch_width = patches.shape
    seen = visible.shape[1]
    rows = -(-seen // 32) * 32
    quarter = patch_width // 4
    width = embed_weight.shape[1]
    head_cols = qkv_weight.shape[2]
    heads = head_cols // HS
    index = jnp.pad(visible, ((0, 0), (0, rows - seen)), constant_values=-1).reshape(clips * rows, 1)
    f32 = jnp.float32
    par = jnp.stack(
        [
            embed_bias.astype(f32), norm_gain.astype(f32),
            jnp.pad(query_gain, (0, width - head_cols)), jnp.pad(key_gain, (0, width - head_cols)),
        ]
    )
    vmem = pl.BlockSpec(memory_space=pltpu.VMEM)
    hbm = pl.BlockSpec(memory_space=pl.ANY)
    bf16 = jnp.bfloat16
    dma = pltpu.SemaphoreType.DMA
    out = pl.pallas_call(
        functools.partial(kernel, (clips, rows, seen, quarter, width, heads)),
        out_shape=jax.ShapeDtypeStruct((clips * rows, head_cols), bf16),
        in_specs=[vmem, vmem, vmem, hbm, hbm, hbm],
        out_specs=vmem,
        scratch_shapes=[
            pltpu.VMEM((clips, tubes, patch_width), bf16),
            pltpu.VMEM((patch_width, width), bf16),
            pltpu.VMEM((3, D, head_cols), bf16),
            pltpu.VMEM((clips, 4, rows, quarter), bf16),
            pltpu.VMEM((clips, 3, rows, quarter), bf16),
            pltpu.VMEM((clips, 4, rows, quarter), bf16),
            pltpu.VMEM((clips, rows, width), f32),
            pltpu.VMEM((clips, 4, rows, width), bf16),
            pltpu.VMEM((clips, 4, 16, 256), f32),
            pltpu.VMEM((4, 1, width), f32),
            pltpu.VMEM((rows, width), bf16),
            pltpu.VMEM((clips, 3, rows, head_cols), f32),
            dma((7,)), dma((3,)), dma((3,)), dma((clips, 3)), dma((clips, 3)),
            dma((clips, 6)), dma((clips, 6)), dma((clips, 3)), dma((clips, 3)),
            dma((clips, 6)), dma((clips, 6)),
        ],
        compiler_params=pltpu.CompilerParams(
            collective_id=0, has_side_effects=True, vmem_limit_bytes=63 * 1024 * 1024
        ),
        name="encoder_block",
    )(index, par, jnp.asarray(turn_table()), patches, embed_weight, jnp.transpose(qkv_weight, (1, 0, 2)))
    return out.reshape(clips, rows, head_cols)[:, :seen]


def solution(mesh):
    local = local_square if mesh.shape["mp"] == 4 else local_generic
    return jax.shard_map(
        local,
        mesh=mesh,
        in_specs=(
            P("dp", "mp", None),
            P("dp", None),
            P(None, "mp"),
            P("mp"),
            P("mp"),
            P(None, None, "mp"),
            P("mp"),
            P("mp"),
        ),
        out_specs=P("dp", None, "mp"),
        check_vma=False,
    )
```

```python
import functools

import jax
import jax.numpy as jnp
import numpy as np
from jax import lax
from jax.experimental import pallas as pl
from jax.experimental.pallas import tpu as pltpu
from jax.sharding import PartitionSpec as P

D = 6144
HS = 128


eps = 1e-06


def positions(index, columns):
    rate = jnp.power(jnp.float32(10000.0), -(2 * (columns // 2)).astype(jnp.float32) / D)
    angle = index.astype(jnp.float32)[..., None] * rate
    return jnp.where(columns % 2 == 0, jnp.sin(angle), jnp.cos(angle))


def normalize(values, gain):
    width = values.shape[-1]
    row_mean = jnp.sum(values, -1, keepdims=True) / width
    row_var = jnp.sum(values * values, -1, keepdims=True) / width - row_mean * row_mean
    return (values - row_mean) * lax.rsqrt(row_var + eps) * gain


def local_generic(patches, visible, embed_weight, embed_bias, norm_gain, qkv_weight, query_gain, key_gain):
    clip_count, local_tubes, patch_width = patches.shape
    seen = visible.shape[1]
    row_count = clip_count * seen
    feature_local = embed_weight.shape[1]
    head_cols = qkv_weight.shape[2]
    heads_local = head_cols // HS
    first_tube = lax.axis_index("mp") * local_tubes
    selector = (
        visible[:, :, None] - first_tube == jnp.arange(local_tubes, dtype=jnp.int32)[None, None, :]
    ).astype(jnp.bfloat16)
    picked = (
        jnp.einsum("cvt,ctp->cvp", selector, patches, preferred_element_type=jnp.float32)
        .reshape(row_count, patch_width)
        .astype(jnp.bfloat16)
    )
    shared = lax.psum(picked, "mp").astype(jnp.float32).astype(jnp.bfloat16)
    embedded = jnp.dot(shared, embed_weight, preferred_element_type=jnp.float32)
    columns = lax.axis_index("mp") * feature_local + jnp.arange(feature_local, dtype=jnp.int32)
    placed = positions(visible, columns).reshape(row_count, feature_local)
    tokens = (embedded + embed_bias.astype(jnp.float32) + placed).astype(jnp.bfloat16)
    weight_flat = qkv_weight.reshape(qkv_weight.shape[0], 3 * head_cols)
    token_float = tokens.astype(jnp.float32)
    row_sums = lax.psum((jnp.sum(token_float, 1), jnp.sum(token_float * token_float, 1)), "mp")
    row_mean = row_sums[0] / D
    row_var = row_sums[1] / D - row_mean * row_mean
    normed = (
        (token_float - row_mean[:, None])
        * lax.rsqrt(row_var + eps)[:, None]
        * norm_gain.astype(jnp.float32)
    ).astype(jnp.bfloat16)
    projected = jnp.dot(
        lax.all_gather(normed, "mp", axis=1, tiled=True),
        weight_flat,
        preferred_element_type=jnp.float32,
    )
    projected = projected.astype(jnp.bfloat16).reshape(clip_count, seen, 3, heads_local, HS)
    queries = projected[:, :, 0].astype(jnp.float32)
    keys_local = projected[:, :, 1].astype(jnp.float32)
    values_local = projected[:, :, 2]
    query_normed = normalize(queries, query_gain.reshape(heads_local, HS)).astype(jnp.bfloat16)
    key_normed = normalize(keys_local, key_gain.reshape(heads_local, HS)).astype(jnp.bfloat16)
    scores = jnp.einsum(
        "cqhd,ckhd->chqk", query_normed, key_normed, preferred_element_type=jnp.float32
    ) / jnp.sqrt(jnp.float32(HS))
    probabilities = jax.nn.softmax(scores, axis=-1).astype(jnp.bfloat16)
    context = jnp.einsum(
        "chqk,ckhd->cqhd", probabilities, values_local, preferred_element_type=jnp.float32
    )
    return context.reshape(clip_count, seen, head_cols).astype(jnp.bfloat16)


MESH = pl.DeviceIdType.MESH
NEG = -1e30


def turn_table():
    columns = np.arange(D)
    turns = 10000.0 ** (-2.0 * (columns // 2) / D) / (2 * np.pi)
    exponent = np.floor(np.log2(turns))
    step = 2.0 ** (exponent - 11)
    high = np.round(turns / step) * step
    low = turns - high
    phase = np.where(columns % 2 == 0, 0.0, 0.25)
    table = np.zeros((8, D), np.float32)
    table[0], table[1], table[2] = high, low, phase
    return table


def sine_of_turns(turn):
    size = jnp.abs(turn)
    size = jnp.minimum(size, 0.5 - size)
    x = jnp.where(turn < 0, -size, size) * jnp.float32(2 * np.pi)
    y = x * x
    s = jnp.float32(2.7557319e-06) - jnp.float32(2.5052108e-08) * y
    s = s * y - jnp.float32(1.9841270e-04)
    s = s * y + jnp.float32(8.3333333e-03)
    s = s * y - jnp.float32(1.6666667e-01)
    return x + x * y * s


def kernel(
    sizes,
    visible_ref, bias_ref, gain_ref, query_gain_ref, key_gain_ref, table_ref, patches_hbm, embed_hbm, qkv_hbm,
    out_ref,
    patch, embed, weight, masked, part, picked, placed, tokens, stats, gains, normed, total, line, index_ref, hop,
    local_sem, gain_send, gain_recv, part_send, part_recv, pick_send, pick_recv,
    stat_send, stat_recv, token_send, token_recv,
):
    clips, rows, seen, quarter, width, heads = sizes
    half = rows // 2
    me = lax.axis_index("mp")
    dp = lax.axis_index("dp")
    xn = me + 1 - 2 * (me % 2)
    yn = me + 2 - 4 * (me // 2)
    dg = 3 - me
    peers = (xn, yn, dg)

    def push(src, dst, send, recv, peer):
        return pltpu.make_async_remote_copy(
            src_ref=src, dst_ref=dst, send_sem=send, recv_sem=recv,
            device_id=(dp, peer), device_id_type=MESH,
        )

    patch_copies = [
        pltpu.make_async_copy(patches_hbm.at[c], patch.at[c], local_sem.at[c]) for c in range(clips)
    ]
    embed_copy = pltpu.make_async_copy(embed_hbm, embed, local_sem.at[2])
    for copy in patch_copies:
        copy.start()
    embed_copy.start()
    barrier = pltpu.get_barrier_semaphore()
    for peer in peers:
        pl.semaphore_signal(barrier, inc=1, device_id=(dp, peer), device_id_type=MESH)
    order = (me, xn, yn, dg)
    weight_copies = []
    for k, s in enumerate(order):
        span = pl.ds(pl.multiple_of(s * width, width), width)
        copy = pltpu.make_async_copy(
            qkv_hbm.at[:, span, :], weight.at[:, span, :], local_sem.at[3 + k]
        )
        copy.start()
        weight_copies.append(copy)
    bias = bias_ref[...].astype(jnp.float32).reshape(1, width)
    query_gain = query_gain_ref[...].reshape(1, heads * HS)
    key_gain = key_gain_ref[...].reshape(1, heads * HS)
    gains[me] = gain_ref[...].astype(jnp.float32).reshape(1, width)
    line[...] = jnp.full(line.shape, -1.0, jnp.float32)
    line[0:clips, 0:seen] = visible_ref[...].astype(jnp.float32)
    upright = jnp.transpose(line[...])
    for c in range(clips):
        index_ref[c * rows:(c + 1) * rows, :] = upright[0:rows, c:c + 1]

    sends = []

    def select(c):
        patch_copies[c].wait()
        tubes = patch.shape[1]
        first = me * tubes
        spot = (lax.broadcasted_iota(jnp.int32, (rows, tubes), 1) + first).astype(jnp.float32)
        pick = (index_ref[pl.ds(c * rows, rows), :] == spot).astype(jnp.float32).astype(jnp.bfloat16)
        for q in range(4):
            masked[c, q] = jnp.dot(
                pick, patch[c, :, q * quarter:(q + 1) * quarter], preferred_element_type=jnp.float32
            ).astype(jnp.bfloat16)

    low, high = pl.ds(0, half), pl.ds(half, half)

    def gather_parts(c):
        def one(k, peer, src, dst):
            return push(src, dst, part_send.at[c, k], part_recv.at[c, k], peer)

        return [
            one(0, xn, masked.at[c, dg, low, :], hop.at[c, 0]),
            one(1, yn, masked.at[c, dg, high, :], hop.at[c, 1]),
            one(2, xn, masked.at[c, xn, low, :], part.at[c, 0, low, :]),
            one(3, yn, masked.at[c, yn, high, :], part.at[c, 1, high, :]),
            one(4, xn, masked.at[c, xn, high, :], part.at[c, 0, high, :]),
            one(5, yn, masked.at[c, yn, low, :], part.at[c, 1, low, :]),
        ]

    part_copies = [gather_parts(c) for c in range(clips)]

    def merge(c):
        part_copies[c][0].wait_recv()
        masked[c, yn, 0:half, :] = masked[c, yn, 0:half, :] + hop[c, 0]
        part_copies[c][5].start()
        part_copies[c][1].wait_recv()
        masked[c, xn, half:rows, :] = masked[c, xn, half:rows, :] + hop[c, 1]
        part_copies[c][4].start()

    def spread(buffer, c, send, recv):
        def one(src, span, k, peer):
            ref = buffer.at[c, src, span, :]
            return push(ref, ref, send.at[c, k], recv.at[c, k], peer)

        own = [one(me, low, 0, xn), one(me, high, 3, yn), one(me, high, 1, xn), one(me, low, 2, yn)]
        forward = {0: one(xn, low, 4, yn), 3: one(yn, high, 5, xn)}
        arrive = [
            one(xn, low, 0, xn), one(xn, high, 1, xn), one(yn, low, 2, yn), one(yn, high, 3, yn),
            one(dg, low, 4, yn), one(dg, high, 5, xn),
        ]
        return own, forward, arrive

    pick_plan = [spread(picked, c, pick_send, pick_recv) for c in range(clips)]
    token_plan = [spread(tokens, c, token_send, token_recv) for c in range(clips)]

    def begin(plan):
        for copy in plan[0]:
            copy.start()

    def relay(plan):
        for k in (0, 3):
            plan[2][k].wait_recv()
            plan[1][k].start()

    select(0)
    pl.semaphore_wait(barrier, 3)
    for copy in part_copies[0][0:4]:
        copy.start()
    gain_copies = [
        push(gains.at[me], gains.at[me], gain_send.at[k], gain_recv.at[k], peer)
        for k, peer in enumerate(peers)
    ]
    for copy in gain_copies:
        copy.start()
    select(1)
    for copy in part_copies[1][0:4]:
        copy.start()

    here = pl.ds(pl.multiple_of(me * width, width), width)
    def place(c):
        @pl.loop(0, rows // 16)
        def _(r):
            span = pl.ds(pl.multiple_of(r * 16, 16), 16)
            vspan = pl.ds(pl.multiple_of(c * rows + r * 16, 16), 16)
            index = index_ref[vspan, :]
            coarse = index * table_ref[0:1, here]
            turn = (coarse - jnp.round(coarse)) + index * table_ref[1:2, here] + table_ref[2:3, here]
            turn = turn - jnp.round(turn)
            placed[c, span, :] = sine_of_turns(turn) + bias

    def collect(c):
        for copy in part_copies[c][2:6]:
            copy.wait_recv()
        picked[c, me] = masked[c, me] + part[c, 0] + part[c, 1]
        begin(pick_plan[c])

    merge(0)
    place(0)
    merge(1)
    collect(0)
    place(1)
    collect(1)

    ones = jnp.ones((8, width), jnp.bfloat16)
    rowdims = (((1,), (1,)), ((), ()))
    stat_copies = [
        [
            push(stats.at[c, me], stats.at[c, me], stat_send.at[c, k], stat_recv.at[c, k], peer)
            for k, peer in enumerate(peers)
        ]
        for c in range(clips)
    ]
    for c in range(clips):
        relay(pick_plan[c])
        for k in (1, 2, 4, 5):
            pick_plan[c][2][k].wait_recv()
        if c == 0:
            embed_copy.wait()
        for n in range(width // 512):
            cols = slice(n * 512, (n + 1) * 512)
            value = placed[c, :, cols]
            for q in range(4):
                value += jnp.dot(
                    picked[c, q], embed[q * quarter:(q + 1) * quarter, cols],
                    preferred_element_type=jnp.float32,
                )
            tokens[c, me, :, cols] = value.astype(jnp.bfloat16)
        begin(token_plan[c])
        value = tokens[c, me]
        wide = value.astype(jnp.float32)
        square = wide * wide
        top = square.astype(jnp.bfloat16)
        rest = (square - top.astype(jnp.float32)).astype(jnp.bfloat16)
        sums = lax.dot_general(ones, value, rowdims, preferred_element_type=jnp.float32)
        squares = lax.dot_general(ones, top, rowdims, preferred_element_type=jnp.float32)
        squares += lax.dot_general(ones, rest, rowdims, preferred_element_type=jnp.float32)
        stats[c, me, 0:8, 0:rows] = sums
        stats[c, me, 8:16, 0:rows] = squares
        for copy in stat_copies[c]:
            copy.start()

    def row_stats(c):
        for copy in stat_copies[c]:
            copy.wait_recv()
        both = (stats[c, 0] + stats[c, 1]) + (stats[c, 2] + stats[c, 3])
        both = both[:, 0:rows]
        mean = both[0:8, :] / D
        scale = lax.rsqrt(both[8:16, :] / D - mean * mean + eps)
        return jnp.transpose(mean)[:, 0:1], jnp.transpose(scale)[:, 0:1]

    def project(c, k, mean, scale):
        s = order[k]
        normed[...] = (
            (tokens[c, s].astype(jnp.float32) - mean) * scale * gains[s]
        ).astype(jnp.bfloat16)
        if c == 0:
            weight_copies[k].wait()
        span = pl.ds(pl.multiple_of(s * width, width), width)
        block = 512
        per = weight.shape[2] // block

        @pl.loop(0, 3 * per)
        def _(t):
            j, n = t // per, t % per
            cols = pl.ds(pl.multiple_of(n * block, block), block)
            value = jnp.dot(normed[...], weight[j, span, cols], preferred_element_type=jnp.float32)
            if k == 0:
                total[c, j, :, cols] = value
            else:
                total[c, j, :, cols] += value

    def head_norm(value, gain):
        value = value.astype(jnp.bfloat16).astype(jnp.float32)
        mean = jnp.sum(value, -1, keepdims=True) / HS
        var = jnp.sum(value * value, -1, keepdims=True) / HS - mean * mean
        return ((value - mean) * lax.rsqrt(var + eps) * gain).astype(jnp.bfloat16)

    valid = lax.broadcasted_iota(jnp.int32, (rows, rows), 1) < seen

    def attend(c):
        for h in range(heads):
            cols = slice(h * HS, (h + 1) * HS)
            query = head_norm(total[c, 0, :, cols], query_gain[:, cols])
            key = head_norm(total[c, 1, :, cols], key_gain[:, cols])
            scores = lax.dot_general(query, key, rowdims, preferred_element_type=jnp.float32)
            scores = jnp.where(valid, scores * jnp.float32(1 / np.sqrt(HS)), NEG)
            weights = jnp.exp(scores - jnp.max(scores, -1, keepdims=True))
            amount = jnp.sum(weights, -1, keepdims=True)
            context = jnp.dot(
                weights.astype(jnp.bfloat16), total[c, 2, :, cols].astype(jnp.bfloat16),
                preferred_element_type=jnp.float32,
            )
            out_ref[c * rows:(c + 1) * rows, cols] = (context / amount).astype(jnp.bfloat16)

    for copy in gain_copies:
        copy.wait_recv()
    mean0, scale0 = row_stats(0)
    project(0, 0, mean0, scale0)
    relay(token_plan[0])
    token_plan[0][2][1].wait_recv()
    project(0, 1, mean0, scale0)
    token_plan[0][2][2].wait_recv()
    project(0, 2, mean0, scale0)
    mean1, scale1 = row_stats(1)
    project(1, 0, mean1, scale1)
    token_plan[0][2][4].wait_recv()
    token_plan[0][2][5].wait_recv()
    relay(token_plan[1])
    project(0, 3, mean0, scale0)
    attend(0)
    token_plan[1][2][1].wait_recv()
    project(1, 1, mean1, scale1)
    token_plan[1][2][2].wait_recv()
    project(1, 2, mean1, scale1)
    token_plan[1][2][4].wait_recv()
    token_plan[1][2][5].wait_recv()
    project(1, 3, mean1, scale1)
    attend(1)

    for copy in gain_copies:
        copy.wait_send()
    for c in range(clips):
        for copy in part_copies[c] + stat_copies[c]:
            copy.wait_send()
        for plan in (pick_plan[c], token_plan[c]):
            for copy in plan[0] + [plan[1][0], plan[1][3]]:
                copy.wait_send()


def local_square(patches, visible, embed_weight, embed_bias, norm_gain, qkv_weight, query_gain, key_gain):
    clips, tubes, patch_width = patches.shape
    seen = visible.shape[1]
    rows = -(-seen // 32) * 32
    quarter = patch_width // 4
    width = embed_weight.shape[1]
    head_cols = qkv_weight.shape[2]
    heads = head_cols // HS
    f32 = jnp.float32
    vmem = pl.BlockSpec(memory_space=pltpu.VMEM)
    hbm = pl.BlockSpec(memory_space=pl.ANY)
    bf16 = jnp.bfloat16
    dma = pltpu.SemaphoreType.DMA
    out = pl.pallas_call(
        functools.partial(kernel, (clips, rows, seen, quarter, width, heads)),
        out_shape=jax.ShapeDtypeStruct((clips * rows, head_cols), bf16),
        in_specs=[vmem] * 6 + [hbm] * 3,
        out_specs=vmem,
        scratch_shapes=[
            pltpu.VMEM((clips, tubes, patch_width), bf16),
            pltpu.VMEM((patch_width, width), bf16),
            pltpu.VMEM((3, D, head_cols), bf16),
            pltpu.VMEM((clips, 4, rows, quarter), bf16),
            pltpu.VMEM((clips, 2, rows, quarter), bf16),
            pltpu.VMEM((clips, 4, rows, quarter), bf16),
            pltpu.VMEM((clips, rows, width), f32),
            pltpu.VMEM((clips, 4, rows, width), bf16),
            pltpu.VMEM((clips, 4, 16, 256), f32),
            pltpu.VMEM((4, 1, width), f32),
            pltpu.VMEM((rows, width), bf16),
            pltpu.VMEM((clips, 3, rows, head_cols), f32),
            pltpu.VMEM((8, -(-rows // 128) * 128), f32),
            pltpu.VMEM((clips * rows, 1), f32),
            pltpu.VMEM((clips, 2, rows // 2, quarter), bf16),
            dma((7,)), dma((3,)), dma((3,)), dma((clips, 6)), dma((clips, 6)),
            dma((clips, 6)), dma((clips, 6)), dma((clips, 3)), dma((clips, 3)),
            dma((clips, 6)), dma((clips, 6)),
        ],
        compiler_params=pltpu.CompilerParams(
            collective_id=0, has_side_effects=True, vmem_limit_bytes=63 * 1024 * 1024
        ),
        name="encoder_block",
    )(
        visible, embed_bias, norm_gain, query_gain, key_gain, jnp.asarray(turn_table()), patches, embed_weight,
        jnp.transpose(qkv_weight, (1, 0, 2)),
    )
    return out.reshape(clips, rows, head_cols)[:, :seen]


def solution(mesh):
    local = local_square if mesh.shape["mp"] == 4 else local_generic
    return jax.shard_map(
        local,
        mesh=mesh,
        in_specs=(
            P("dp", "mp", None),
            P("dp", None),
            P(None, "mp"),
            P("mp"),
            P("mp"),
            P(None, None, "mp"),
            P("mp"),
            P("mp"),
        ),
        out_specs=P("dp", None, "mp"),
        check_vma=False,
    )
```
